256 devices in a mesh: row: 32 (over z_lo, x, core), col: 8 (over y, z_hi).
Axes of the slice: x: 4, y: 4, z: 8 (z_hi: 2, z_lo: 4; z = z_hi * 4 + z_lo), core: 2. Of those that a mesh axis runs over, the one named last changes fastest.
Arguments:
- vectors: bfloat16 [8, 32768], P(None, ('row', 'col')), may hold values from -16 to 16, as said below
- tile_vals: bfloat16 [32, 8, 3, 32, 128, 128], P('row', 'col'), may hold values from -0.125 to 0.125
- tile_rows: int32 [32, 8, 3, 32], P('row', 'col'), may hold values from 0 to 7, as said below
- tile_cols: int32 [32, 8, 3, 32], P('row', 'col'), may hold values from 0 to 31, as said below
- tile_counts: int32 [32, 8, 3], P('row', 'col'), may hold values from 1 to 32, as said below
- tile_diag: int32 [32, 8, 3, 32], P('row', 'col'), may hold values from 0 to 1, as said below
Outputs:
- applied: float32 [3, 8, 32768], P(None, None, ('row', 'col'))
- subspace: float32 [3, 8, 8], replicated
The draws below stay inside these ranges and needn't reach their ends.
Inputs may be any that keep to these rules, and one draw needn't show every extreme that they name: `vectors`: eigenvector amplitudes vary over the basis. `tile_rows`: the first tile_counts slots of a term on a device name distinct tiles whose global tile row is at least the global tile column; later slots are ignored. `tile_cols`: see tile_rows. `tile_counts`: loads differ from device to device. `tile_diag`: 1 exactly for live slots whose global tile row equals the global tile column, else 0.
All inputs are finite; a program needn't handle non-finite values.
Results may differ from the reference program's by a relative error of at most 0.0003.
Values may be sent and summed in bfloat16 or wider, within the bound.
No kernel may reach another device: no remote copies, remote signals or barrier semaphores. Data moves between devices by JAX's collectives and lax.ppermute only.
A program may use at most 64 MiB of HBM per device.

```python
import math
import jax
import jax.numpy as jnp
from jax import lax

EV = 8
NTERM = 3
TILE = 128
PT = 1
GR = 32
GC = 8
K = 32
N = 32768


def layout_draw(key):
    layout_key = jax.random.fold_in(key, 7)
    first_key = jax.random.fold_in(layout_key, 1)
    second_key = jax.random.fold_in(layout_key, 2)
    row_tiles = GC * PT
    col_tiles = GR * PT
    places = row_tiles * col_tiles
    grid_r = jnp.arange(GR, dtype=jnp.int32)[:, None, None]
    grid_c = jnp.arange(GC, dtype=jnp.int32)[None, :, None]
    position = jnp.arange(places, dtype=jnp.int32)
    local_a = position // col_tiles
    local_b = position % col_tiles
    glob_row = (grid_r * GC + local_a // PT) * PT + local_a % PT
    glob_col = (local_b // PT * GC + grid_c) * PT + local_b % PT
    lower = glob_row >= glob_col
    avail = jnp.sum(lower.astype(jnp.int32), axis=-1)
    peak = jnp.max(avail)
    density = jax.random.randint(first_key, (GR, GC, NTERM), 8, 17, dtype=jnp.int32)
    scaled = jnp.maximum(1, K * avail[:, :, None] * density // (8 * peak))
    counts = jnp.minimum(jnp.minimum(K, avail[:, :, None]), scaled).astype(jnp.int32)
    upper_score = max(1, 2 ** 30 // places)
    scores = jax.random.randint(second_key, (GR, GC, NTERM, places), 0, upper_score, dtype=jnp.int32)
    keyed = jnp.where(lower[:, :, None, :], scores * places + position, 2 ** 30 + position)
    order = jnp.argsort(keyed, axis=-1)[..., :K].astype(jnp.int32)
    rows_sel = order // col_tiles
    cols_sel = order % col_tiles
    live = jnp.arange(K, dtype=jnp.int32)[None, None, None, :] < counts[..., None]
    grid_r4 = jnp.arange(GR, dtype=jnp.int32)[:, None, None, None]
    grid_c4 = jnp.arange(GC, dtype=jnp.int32)[None, :, None, None]
    sel_row = (grid_r4 * GC + rows_sel // PT) * PT + rows_sel % PT
    sel_col = (cols_sel // PT * GC + grid_c4) * PT + cols_sel % PT
    flags = jnp.where(live & (sel_row == sel_col), 1, 0).astype(jnp.int32)
    return (rows_sel, cols_sel, counts, flags)


def draw_tile_rows(key, part):
    return layout_draw(key)[0]


def draw_tile_cols(key, part):
    return layout_draw(key)[1]


def draw_tile_counts(key, part):
    return layout_draw(key)[2]


def draw_tile_diag(key, part):
    return layout_draw(key)[3]


def draw_vectors(key, part):
    total = TILE * PT * GR * GC
    place = jnp.arange(total, dtype=jnp.float32) / total
    base = jnp.clip(jax.random.normal(key, (EV, total), jnp.float32), -4.0, 4.0)
    amplitude = jnp.exp(jnp.log(3.0) * place)
    return (base * amplitude[None, :]).astype(jnp.bfloat16)


def shard_levels(stream_key, shape, cuts, least, high):
    gain = 1.0
    for dim, parts in cuts:
        draws = jax.random.uniform(jax.random.fold_in(jax.random.fold_in(stream_key, 6), dim), (parts,), jnp.float32, least / len(cuts), high / len(cuts))
        gain = gain * jnp.repeat(jnp.exp(draws), shape[dim] // parts).reshape((-1,) + (1,) * (len(shape) - 1 - dim))
    return gain


def normal_values(own_key, dims, deviation, bound, cuts=(), kind=jnp.bfloat16):
    drawn = jax.random.normal(own_key, dims, jnp.float32) * deviation
    if len(cuts) > 0:
        drawn = shard_levels(own_key, dims, cuts, -0.22, 0.18) * drawn
    return jnp.clip(drawn, min=-bound, max=bound).astype(kind)


def setup_inputs(seed: int = 0) -> dict:
    streams_of = jax.random.split(jax.random.key(seed), 7)
    vectors = draw_vectors(jax.random.fold_in(streams_of[6], 71), 0)
    tile_vals = normal_values(streams_of[1], (GR, GC, NTERM, K, TILE, TILE), (64 * K) ** -0.5, 0.125, ((0, 32), (1, 8)))
    tile_rows = draw_tile_rows(jax.random.fold_in(streams_of[6], 71), 0)
    tile_cols = draw_tile_cols(jax.random.fold_in(streams_of[6], 71), 0)
    tile_counts = draw_tile_counts(jax.random.fold_in(streams_of[6], 71), 0)
    tile_diag = draw_tile_diag(jax.random.fold_in(streams_of[6], 71), 0)
    return dict(vectors=vectors, tile_vals=tile_vals, tile_rows=tile_rows, tile_cols=tile_cols, tile_counts=tile_counts, tile_diag=tile_diag)


def reference(vectors, tile_vals, tile_rows, tile_cols, tile_counts, tile_diag):
    values = vectors.astype(jnp.float32)
    segments = values.reshape(EV, N // TILE, TILE)
    applied = jnp.zeros((NTERM, EV, N // TILE, TILE), jnp.float32)
    slot_ids = jnp.arange(K, dtype=jnp.int32)

    def device_step(index, applied):
        grid_r = (index // GC).astype(jnp.int32)
        grid_c = (index % GC).astype(jnp.int32)
        for term_idx in range(NTERM):
            tiles_now = tile_vals[grid_r, grid_c, term_idx].astype(jnp.float32)
            rows_now = tile_rows[grid_r, grid_c, term_idx].astype(jnp.int32)
            cols_now = tile_cols[grid_r, grid_c, term_idx].astype(jnp.int32)
            live_wt = (slot_ids < tile_counts[grid_r, grid_c, term_idx]).astype(jnp.float32)
            mirror_wt = live_wt * (1 - tile_diag[grid_r, grid_c, term_idx]).astype(jnp.float32)
            glob_row = ((grid_r * GC + rows_now // PT) * PT + rows_now % PT).astype(jnp.int32)
            glob_col = ((cols_now // PT * GC + grid_c) * PT + cols_now % PT).astype(jnp.int32)
            forward_terms = jnp.einsum('kij,ekj->eki', tiles_now, segments[:, glob_col], precision=lax.Precision.HIGHEST)
            forward_terms = forward_terms * live_wt[None, :, None]
            mirror_terms = jnp.einsum('kij,eki->ekj', tiles_now, segments[:, glob_row], precision=lax.Precision.HIGHEST)
            mirror_terms = mirror_terms * mirror_wt[None, :, None]
            term_slab = applied[term_idx]
            term_slab = term_slab.at[:, glob_row].add(forward_terms)
            term_slab = term_slab.at[:, glob_col].add(mirror_terms)
            applied = applied.at[term_idx].set(term_slab)
        return applied
    applied = lax.fori_loop(0, GR * GC, device_step, applied)
    applied = applied.reshape(NTERM, EV, N)
    raw = jnp.einsum('ei,tfi->tef', values, applied, precision=lax.Precision.HIGHEST)
    return (applied, raw / math.sqrt(N))
```

```python
import math

import jax
import jax.numpy as jnp
from jax import lax
from jax.experimental import pallas as pl
from jax.experimental.pallas import tpu as pltpu
from jax.sharding import PartitionSpec as P

ROW = "row"
COL = "col"
GROUP = 8


def dot_cols(x, w):
    return lax.dot_general(x, w, (((1,), (1,)), ((), ())), preferred_element_type=jnp.float32)


def dot_rows(x, w):
    return lax.dot_general(x, w, (((1,), (0,)), ((), ())), preferred_element_type=jnp.float32)


def tiles_kernel(rows, cols, counts, diag, row_segs, col_segs, tiles, fwd, mir):
    terms, slots = rows.shape
    vecs = row_segs.shape[1]
    fwd[...] = jnp.zeros_like(fwd)
    mir[...] = jnp.zeros_like(mir)
    for t in range(terms):
        count = counts[0, t]

        @pl.loop(0, (count + GROUP - 1) // GROUP)
        def _(g):
            outs = []
            for u in range(GROUP):
                k = g * GROUP + u
                a = rows[t, k]
                b = cols[t, k]
                w = tiles[t, k]
                y = dot_cols(col_segs[b], w)
                z = dot_rows(row_segs[a], w)
                outs.append((k, a, b, y, z))
            for k, a, b, y, z in outs:
                live = k < count
                both = jnp.logical_and(live, diag[t, k] == 0)
                at = pl.ds(t * vecs, vecs)
                fwd[a, at, :] += jnp.where(live, y, 0.0)
                mir[b, at, :] += jnp.where(both, z, 0.0)

    total = jnp.zeros((vecs, 2 * terms * vecs), jnp.float32)
    span = terms * vecs
    for segs, sums in ((row_segs, fwd), (col_segs, mir)):
        for s in range(segs.shape[0]):
            part = sums[s, :span, :]
            high = part.astype(jnp.bfloat16)
            low = (part - high.astype(jnp.float32)).astype(jnp.bfloat16)
            total += dot_cols(segs[s], jnp.concatenate([high, low], axis=0))
    small = total[:, :span] + total[:, span:]
    small = jnp.concatenate([small, jnp.zeros((vecs, fwd.shape[2] - span), jnp.float32)], axis=1)
    for s in range(fwd.shape[0]):
        fwd[s, span : span + vecs, :] = small


def apply_tiles(rows, cols, counts, diag, row_segs, col_segs, tiles):
    terms = tiles.shape[0]
    vecs, width = row_segs.shape[1:]
    height = (terms + 1) * vecs
    smem = pl.BlockSpec(memory_space=pltpu.SMEM)
    vmem = pl.BlockSpec(memory_space=pltpu.VMEM)
    return pl.pallas_call(
        tiles_kernel,
        out_shape=(
            jax.ShapeDtypeStruct((row_segs.shape[0], height, width), jnp.float32),
            jax.ShapeDtypeStruct((col_segs.shape[0], height, width), jnp.float32),
        ),
        in_specs=[smem] * 4 + [vmem] * 3,
        out_specs=(vmem, vmem),
        compiler_params=pltpu.CompilerParams(vmem_limit_bytes=16 * 1024 * 1024),
    )(rows, cols, counts, diag, row_segs, col_segs, tiles)


def exchange(value, axis):
    return lax.all_to_all(value, axis, 0, 0, tiled=True)


def gather(value, axis):
    return exchange(jnp.broadcast_to(value, (lax.axis_size(axis), *value.shape)), axis)


def shards(vectors, tile_vals, tile_rows, tile_cols, tile_counts, tile_diag):
    vecs, width = vectors.shape
    terms = tile_vals.shape[2]
    span = terms * vecs
    row_segs = gather(vectors, COL)
    col_segs = gather(vectors, ROW)
    fwd, mir = apply_tiles(
        tile_rows[0, 0],
        tile_cols[0, 0],
        tile_counts[0],
        tile_diag[0, 0],
        row_segs,
        col_segs,
        tile_vals[0, 0],
    )
    fwd = jnp.sum(exchange(fwd, COL), axis=0)
    mir = lax.dynamic_update_slice(
        mir, jnp.broadcast_to(fwd[span:], (mir.shape[0], vecs, width)), (0, span, 0)
    )
    mir = jnp.sum(exchange(mir, ROW), axis=0)
    applied = (fwd[:span] + mir[:span]).reshape(terms, vecs, width)
    small = mir[span:, :span].reshape(vecs, terms, vecs).transpose(1, 0, 2)
    states = width * lax.axis_size(ROW) * lax.axis_size(COL)
    return applied, small / math.sqrt(states)


def solution(mesh):
    grid = P(ROW, COL)
    return jax.shard_map(
        shards,
        mesh=mesh,
        in_specs=(P(None, (ROW, COL)), grid, grid, grid, grid, grid),
        out_specs=(P(None, None, (ROW, COL)), P()),
        check_vma=False,
    )
```

```python
import math

import jax
import jax.numpy as jnp
from jax import lax
from jax.experimental import pallas as pl
from jax.experimental.pallas import tpu as pltpu
from jax.sharding import Mesh
from jax.sharding import PartitionSpec as P

ZLOW, ACROSS, CORE, UP, ZHIGH = "zlow", "across", "core", "up", "zhigh"
ROW = (ZLOW, ACROSS, CORE)
CHIPS = (ZLOW, ACROSS)
COL = (UP, ZHIGH)
GROUP = 8


def dot_cols(x, w):
    return lax.dot_general(x, w, (((1,), (1,)), ((), ())), preferred_element_type=jnp.float32)


def dot_rows(x, w):
    return lax.dot_general(x, w, (((1,), (0,)), ((), ())), preferred_element_type=jnp.float32)


def tiles_kernel(codes, row_segs, col_segs, stored, fwd, mir, mir_away, tiles, sems):
    terms, slots = tiles.shape[:2]
    vecs = row_segs.shape[1]
    chips = mir.shape[0]

    def fetch(t, g):
        at = pl.ds(g * GROUP, GROUP)
        return pltpu.make_async_copy(stored.at[t, at], tiles.at[t, at], sems.at[t, g])

    counts = [codes[t, slots] for t in range(terms)]
    for t in range(terms):
        for g in range(slots // GROUP):

            @pl.when(g * GROUP < counts[t])
            def _():
                fetch(t, g).start()

    fwd[...] = jnp.zeros_like(fwd)
    mir[...] = jnp.zeros_like(mir)
    mir_away[...] = jnp.zeros_like(mir_away)
    for t in range(terms):
        count = counts[t]

        @pl.loop(0, (count + GROUP - 1) // GROUP)
        def _(g):
            fetch(t, g).wait()
            outs = []
            for u in range(GROUP):
                k = g * GROUP + u
                code = codes[t, k]
                a = code & 7
                b = (code >> 6) & 31
                w = tiles[t, k]
                y = dot_cols(col_segs[b], w)
                z = dot_rows(row_segs[(code >> 3) & 7], w)
                outs.append((k, code, a, b, y, z))
            for k, code, a, b, y, z in outs:
                live = k < count
                both = jnp.logical_and(live, (code >> 11) == 0)
                at = pl.ds(t * vecs, vecs)
                fwd[a, at, :] += jnp.where(live, y, 0.0)
                z = jnp.where(both, z, 0.0)
                away = b & 1

                @pl.when(away == 0)
                def _():
                    mir[b >> 1, at, :] += z

                @pl.when(away == 1)
                def _():
                    mir_away[b >> 1, at, :] += z

    span = terms * vecs
    group = codes[0, slots + 1]
    total = jnp.zeros((vecs, 2 * span), jnp.float32)

    def products(seg, part):
        high = part.astype(jnp.bfloat16)
        low = (part - high.astype(jnp.float32)).astype(jnp.bfloat16)
        return dot_cols(seg, jnp.concatenate([high, low], axis=0))

    for a in range(fwd.shape[0]):
        total += products(row_segs[(a ^ ((a & 4) >> 1)) ^ group], fwd[a, :span, :])
    for s in range(chips):
        total += products(col_segs[2 * s], mir[s, :span, :])
        total += products(col_segs[2 * s + 1], mir_away[s, :span, :])
    small = total[:, :span] + total[:, span:]
    small = jnp.concatenate([small, jnp.zeros((vecs, fwd.shape[2] - span), jnp.float32)], axis=1)
    for s in range(chips):
        mir[s, span:, :] = small
        mir_away[s, span:, :] = small


def apply_tiles(codes, row_segs, col_segs, tiles):
    terms, slots = tiles.shape[:2]
    vecs, width = row_segs.shape[1:]
    height = (terms + 1) * vecs
    chips = col_segs.shape[0] // 2
    smem = pl.BlockSpec(memory_space=pltpu.SMEM)
    vmem = pl.BlockSpec(memory_space=pltpu.VMEM)
    return pl.pallas_call(
        tiles_kernel,
        out_shape=(
            jax.ShapeDtypeStruct((row_segs.shape[0], height, width), jnp.float32),
            jax.ShapeDtypeStruct((chips, height, width), jnp.float32),
            jax.ShapeDtypeStruct((chips, height, width), jnp.float32),
        ),
        in_specs=[smem, vmem, vmem, pl.BlockSpec(memory_space=pltpu.HBM)],
        out_specs=(vmem, vmem, vmem),
        scratch_shapes=[
            pltpu.VMEM(tiles.shape, tiles.dtype),
            pltpu.SemaphoreType.DMA((terms, slots // GROUP)),
        ],
        compiler_params=pltpu.CompilerParams(vmem_limit_bytes=40 * 1024 * 1024),
    )(codes, row_segs, col_segs, tiles)


def exchange(value, axis):
    return lax.all_to_all(value, axis, 0, 0, tiled=True)


def swap_pairs(value, axis):
    return lax.ppermute(value, axis, [(i, i ^ 1) for i in range(lax.axis_size(axis))])


def swap_ends(value, axis):
    last = lax.axis_size(axis) - 1
    return lax.ppermute(value, axis, [(i, last - i) for i in range(last + 1)])


def doubled(value, swap, axis):
    return jnp.concatenate([value, swap(value, axis)], axis=0)


def shards(vectors, tile_vals, tile_rows, tile_cols, tile_counts, tile_diag):
    vecs, width = vectors.shape
    terms = tile_vals.shape[2]
    span = terms * vecs
    own = vectors[None]
    chips = lax.axis_size(CHIPS)
    pair = doubled(own, swap_pairs, CORE)
    col_segs = exchange(jnp.broadcast_to(pair, (chips, *pair.shape)), CHIPS)
    col_segs = col_segs.reshape(2 * chips, vecs, width)
    row_segs = doubled(own, swap_pairs, ZHIGH)
    row_segs = doubled(row_segs, swap_pairs, UP)
    row_segs = doubled(row_segs, swap_ends, UP)
    up = lax.axis_index(UP)
    group = ((up ^ (up >> 1)) << 1) | lax.axis_index(ZHIGH)
    rows = tile_rows[0, 0]
    codes = (
        rows
        | ((rows ^ ((rows & 4) >> 1) ^ group) << 3)
        | ((tile_cols[0, 0] ^ lax.axis_index(CORE)) << 6)
        | (tile_diag[0, 0] << 11)
    )
    more = jnp.stack([tile_counts[0, 0], jnp.broadcast_to(group, (terms,))], axis=1)
    codes = jnp.concatenate([codes, more.astype(jnp.int32)], axis=1)
    fwd, mir, mir_away = apply_tiles(codes, row_segs, col_segs, tile_vals[0, 0])
    mir = mir + swap_pairs(mir_away, CORE)
    mir = jnp.sum(exchange(mir, CHIPS), axis=0)
    fwd = lax.dynamic_update_slice(
        fwd, jnp.broadcast_to(mir[span:], (fwd.shape[0], vecs, width)), (0, span, 0)
    )
    fwd = jnp.sum(exchange(fwd, COL), axis=0)
    applied = (fwd[:span] + mir[:span]).reshape(terms, vecs, width)
    small = fwd[span:, :span].reshape(vecs, terms, vecs).transpose(1, 0, 2)
    states = width * lax.axis_size(ROW) * lax.axis_size(COL)
    return applied, small / math.sqrt(states)


def solution(mesh):
    torus = Mesh(mesh.devices.reshape(4, 4, 2, 4, 2), ROW + COL)
    grid = P(ROW, COL)
    return jax.shard_map(
        shards,
        mesh=torus,
        in_specs=(P(None, ROW + COL), grid, grid, grid, grid, grid),
        out_specs=(P(None, None, ROW + COL), P()),
        check_vma=False,
    )
```

```python
import math

import jax
import jax.numpy as jnp
from jax import lax
from jax.experimental import pallas as pl
from jax.experimental.pallas import tpu as pltpu
from jax.sharding import Mesh
from jax.sharding import PartitionSpec as P

ZLOW, ACROSS, CORE, UP, ZHIGH = "zlow", "across", "core", "up", "zhigh"
ROW = (ZLOW, ACROSS, CORE)
CHIPS = (ZLOW, ACROSS)
COL = (UP, ZHIGH)
GROUP = 8
SMEM = pl.BlockSpec(memory_space=pltpu.SMEM)
VMEM = pl.BlockSpec(memory_space=pltpu.VMEM)


def in_vmem(value):
    return pltpu.with_memory_space_constraint(value, pltpu.VMEM)


def dot_cols(x, w):
    return lax.dot_general(x, w, (((1,), (1,)), ((), ())), preferred_element_type=jnp.float32)


def dot_rows(x, w):
    return lax.dot_general(x, w, (((1,), (0,)), ((), ())), preferred_element_type=jnp.float32)


def spread_kernel(own, other, pairs, kept):
    kept[0] = own[...]
    for s in range(pairs.shape[0]):
        pairs[s, 0] = own[...]
        pairs[s, 1] = other[0]


def spread(own, other, copies):
    return pl.pallas_call(
        spread_kernel,
        out_shape=(
            pltpu.VMEM((copies, 2, *own.shape), own.dtype),
            pltpu.VMEM((1, *own.shape), own.dtype),
        ),
        in_specs=[VMEM] * 2,
        out_specs=(VMEM, VMEM),
        compiler_params=pltpu.CompilerParams(vmem_limit_bytes=1024 * 1024),
    )(own, in_vmem(other))


def load_kernel(codes, stored, tiles, sems):
    terms, slots = tiles.shape[:2]

    def for_live(act):
        for t in range(terms):
            for g in range(slots // GROUP):

                @pl.when(g * GROUP < codes[terms, 0, t])
                def _():
                    at = pl.ds(g * GROUP, GROUP)
                    act(pltpu.make_async_copy(stored.at[t, at], tiles.at[t, at], sems.at[t, g]))

    for_live(lambda copy: copy.start())
    for_live(lambda copy: copy.wait())


def load_tiles(codes, tiles):
    terms, slots = tiles.shape[:2]
    return pl.pallas_call(
        load_kernel,
        out_shape=pltpu.VMEM(tiles.shape, tiles.dtype),
        in_specs=[SMEM, pl.BlockSpec(memory_space=pltpu.HBM)],
        out_specs=VMEM,
        scratch_shapes=[pltpu.SemaphoreType.DMA((terms, slots // GROUP))],
        compiler_params=pltpu.CompilerParams(vmem_limit_bytes=1024 * 1024),
    )(codes, pltpu.with_memory_space_constraint(tiles, pltpu.HBM))


def for_slots(codes, tiles, work):
    terms, slots = tiles.shape[:2]
    for t in range(terms):
        count = codes[terms, 0, t]

        @pl.loop(0, (count + GROUP - 1) // GROUP)
        def _(g):
            outs = []
            for u in range(GROUP):
                k = g * GROUP + u
                outs.append(work(codes[t, 0, k], tiles[t, k]))
            for ref, at, value in outs:
                ref[at, pl.ds(t * value.shape[0], value.shape[0]), :] += value


def mirror_kernel(codes, row_segs, col_segs, tiles, mir, mir_away, sums):
    terms = tiles.shape[0]
    vecs = row_segs.shape[1]
    chips = mir.shape[0]
    span = terms * vecs
    sums[...] = jnp.zeros_like(sums)
    for_slots(
        codes,
        tiles,
        lambda code, w: (sums, (code >> 8) & 63, dot_rows(row_segs[code & 7], w)),
    )

    def products(seg, part):
        high = part.astype(jnp.bfloat16)
        low = (part - high.astype(jnp.float32)).astype(jnp.bfloat16)
        return dot_cols(seg, jnp.concatenate([high, low], axis=0))

    total = jnp.zeros((vecs, 2 * span), jnp.float32)
    for h, out in enumerate((mir, mir_away)):
        for s in range(chips):
            part = sums[h * chips + s]
            out[s, :span, :] = part
            total += products(col_segs[2 * s + h], part)
    square = products(row_segs[0], sums[2 * chips])
    small = jnp.concatenate(
        [
            total[:, :span] + total[:, span:],
            square[:, :span] + square[:, span:],
            jnp.zeros((vecs, mir.shape[2] - 2 * span), jnp.float32),
        ],
        axis=1,
    )
    for s in range(chips):
        mir[s, span:, :] = small
        mir_away[s, span:, :] = small


def forward_kernel(codes, col_segs, tiles, fwd, sums):
    span = sums.shape[1]
    sums[...] = jnp.zeros_like(sums)
    for_slots(
        codes,
        tiles,
        lambda code, w: (sums, code >> 14, dot_cols(col_segs[(code >> 3) & 31], w)),
    )
    fwd[:, :span, :] = sums[: fwd.shape[0]]
    fwd[:, span:, :] = jnp.zeros_like(fwd[:, span:, :])


def apply_mirror(codes, row_segs, col_segs, tiles):
    terms = tiles.shape[0]
    vecs, width = row_segs.shape[1:]
    chips = col_segs.shape[0] // 2
    out = pltpu.VMEM((chips, (terms + 1) * vecs, width), jnp.float32)
    return pl.pallas_call(
        mirror_kernel,
        out_shape=(out, out),
        in_specs=[SMEM] + [VMEM] * 3,
        out_specs=(VMEM, VMEM),
        scratch_shapes=[pltpu.VMEM((2 * chips + 2, terms * vecs, width), jnp.float32)],
        compiler_params=pltpu.CompilerParams(vmem_limit_bytes=4 * 1024 * 1024),
    )(codes, in_vmem(row_segs), in_vmem(col_segs), in_vmem(tiles))


def apply_forward(codes, col_segs, tiles, pieces):
    terms = tiles.shape[0]
    vecs, width = col_segs.shape[1:]
    return pl.pallas_call(
        forward_kernel,
        out_shape=pltpu.VMEM((pieces, (terms + 1) * vecs, width), jnp.float32),
        in_specs=[SMEM] + [VMEM] * 2,
        out_specs=VMEM,
        scratch_shapes=[pltpu.VMEM((pieces + 1, terms * vecs, width), jnp.float32)],
        compiler_params=pltpu.CompilerParams(vmem_limit_bytes=4 * 1024 * 1024),
    )(codes, in_vmem(col_segs), in_vmem(tiles))


def exchange(value, axis):
    return lax.all_to_all(value, axis, 0, 0, tiled=True)


def swap_pairs(value, axis):
    return lax.ppermute(value, axis, [(i, i ^ 1) for i in range(lax.axis_size(axis))])


def swap_ends(value, axis):
    last = lax.axis_size(axis) - 1
    return lax.ppermute(value, axis, [(i, last - i) for i in range(last + 1)])


def slot_codes(rows, cols, counts, diag, chips, pieces):
    rows, cols, diag = (jnp.transpose(x[0], (1, 0, 2)) for x in (rows, cols, diag))
    terms, _, slots = rows.shape
    up = lax.axis_index(UP)
    group = ((up ^ (up >> 1)) << 1) | lax.axis_index(ZHIGH)
    slot = lax.broadcasted_iota(jnp.int32, rows.shape, 2)
    live = slot < counts[0, 0][:, None, None]
    near = rows ^ ((rows & 4) >> 1) ^ group
    far = cols ^ lax.axis_index(CORE)
    mirrored = jnp.where(diag == 1, 2 * chips, (far & 1) * chips + (far >> 1))
    mirrored = jnp.where(live, mirrored, 2 * chips + 1)
    forward = jnp.where(live, rows, pieces)
    codes = near | (far << 3) | (mirrored << 8) | (forward << 14)
    last = jnp.pad(counts, ((0, 0), (0, 0), (0, slots - terms)))
    return jnp.concatenate([codes, last], axis=0)


def shards(vectors, tile_vals, tile_rows, tile_cols, tile_counts, tile_diag):
    vecs, width = vectors.shape
    terms = tile_vals.shape[2]
    span = terms * vecs
    chips = lax.axis_size(CHIPS)
    pieces = lax.axis_size(COL)

    beyond = swap_pairs(vectors[None], ZHIGH)
    pairs, own = spread(vectors, swap_pairs(vectors[None], CORE), chips)
    col_segs = exchange(pairs, CHIPS)
    row_segs = jnp.concatenate([own, beyond], axis=0)
    col_segs, *index = lax.optimization_barrier(
        (col_segs, tile_rows, tile_cols, tile_counts, tile_diag)
    )
    arrived = swap_pairs(row_segs, UP)
    codes = slot_codes(*index, chips, pieces)
    tiles = load_tiles(codes, tile_vals[0, 0])
    row_segs = jnp.concatenate([row_segs, arrived], axis=0)
    row_segs, col_segs, codes, tiles = lax.optimization_barrier((row_segs, col_segs, codes, tiles))
    col_segs = col_segs.reshape(2 * chips, vecs, width)
    arrived = swap_ends(row_segs, UP)
    fwd = apply_forward(codes, col_segs, tiles, pieces)
    fwd, arrived = lax.optimization_barrier((fwd, arrived))
    row_segs = jnp.concatenate([row_segs, arrived], axis=0)

    mir, mir_away = apply_mirror(codes, row_segs, col_segs, tiles)
    mir = mir + swap_pairs(mir_away, CORE)
    mir = jnp.sum(exchange(mir, CHIPS), axis=0)
    fwd = lax.dynamic_update_slice(
        fwd, jnp.broadcast_to(mir[span:], (pieces, vecs, width)), (0, span, 0)
    )
    fwd = jnp.sum(exchange(fwd, COL), axis=0)
    applied = (fwd[:span] + mir[:span]).reshape(terms, vecs, width)
    small = fwd[span:, : 2 * span].reshape(vecs, 2, terms, vecs)
    small = small[:, 0].transpose(1, 0, 2) + (small[:, 0] + small[:, 1]).transpose(1, 2, 0)
    states = width * lax.axis_size(ROW) * lax.axis_size(COL)
    return applied, small / math.sqrt(states)


def solution(mesh):
    torus = Mesh(mesh.devices.reshape(4, 4, 2, 4, 2), ROW + COL)
    grid = P(ROW, COL)
    return jax.shard_map(
        shards,
        mesh=torus,
        in_specs=(P(None, ROW + COL), grid, grid, grid, grid, grid),
        out_specs=(P(None, None, ROW + COL), P()),
        check_vma=False,
    )
```

```python
import functools
import math

import jax
import jax.numpy as jnp
from jax import lax
from jax.experimental import pallas as pl
from jax.experimental.pallas import tpu as pltpu
from jax.sharding import Mesh
from jax.sharding import PartitionSpec as P

ZLOW, ACROSS, CORE, UP, ZHIGH = "zlow", "across", "core", "up", "zhigh"
ROW = (ZLOW, ACROSS, CORE)
CHIPS = (ZLOW, ACROSS)
COL = (UP, ZHIGH)
GROUP = 8
SMEM = pl.BlockSpec(memory_space=pltpu.SMEM)
VMEM = pl.BlockSpec(memory_space=pltpu.VMEM)


def in_vmem(value):
    return pltpu.with_memory_space_constraint(value, pltpu.VMEM)


def dot_cols(x, w):
    return lax.dot_general(x, w, (((1,), (1,)), ((), ())), preferred_element_type=jnp.float32)


def dot_rows(x, w):
    return lax.dot_general(x, w, (((1,), (0,)), ((), ())), preferred_element_type=jnp.float32)


def spread_kernel(own, other, pairs, kept):
    kept[0] = own[...]
    for s in range(pairs.shape[0]):
        pairs[s, 0] = own[...]
        pairs[s, 1] = other[0]


def spread(own, other, copies):
    return pl.pallas_call(
        spread_kernel,
        out_shape=(
            pltpu.VMEM((copies, 2, *own.shape), own.dtype),
            pltpu.VMEM((1, *own.shape), own.dtype),
        ),
        in_specs=[VMEM] * 2,
        out_specs=(VMEM, VMEM),
        compiler_params=pltpu.CompilerParams(vmem_limit_bytes=1024 * 1024),
    )(own, in_vmem(other))


def load_kernel(
    chips, pieces, where, after, rows, cols, counts, diag, stored, tiles, codes, live, index, sems, done
):
    terms, slots = tiles.shape[:2]
    small = [
        pltpu.make_async_copy(counts, live, done.at[0]),
        pltpu.make_async_copy(rows, index.at[0], done.at[1]),
        pltpu.make_async_copy(cols, index.at[1], done.at[2]),
        pltpu.make_async_copy(diag, index.at[2], done.at[3]),
    ]
    for copy in small:
        copy.start()
    small[0].wait()

    def for_live(act):
        for t in range(terms):
            for g in range(slots // GROUP):

                @pl.when(g * GROUP < live[0, 0, t])
                def _():
                    at = pl.ds(g * GROUP, GROUP)
                    act(pltpu.make_async_copy(stored.at[t, at], tiles.at[t, at], sems.at[t, g]))

    for_live(lambda copy: copy.start())
    for copy in small[1:]:
        copy.wait()
    slot = lax.broadcasted_iota(jnp.int32, (1, slots), 1)
    last = jnp.zeros((1, slots), jnp.int32)
    for t in range(terms):
        row, col, same = (index[n, t] for n in range(3))
        used = slot < live[0, 0, t]
        near = row ^ ((row & 4) >> 1) ^ where[0]
        far = col ^ where[1]
        mirrored = jnp.where(same == 1, 2 * chips, (far & 1) * chips + (far >> 1))
        mirrored = jnp.where(used, mirrored, 2 * chips + 1)
        forward = jnp.where(used, row, pieces)
        codes[t] = near | (far << 3) | (mirrored << 8) | (forward << 14)
        last = jnp.where(slot == t, live[0, 0, t], last)
    codes[terms] = last
    for_live(lambda copy: copy.wait())


def load_tiles(chips, pieces, after, rows, cols, counts, diag, tiles):
    terms, slots = tiles.shape[:2]
    rows, cols, diag = (jnp.transpose(x[0], (1, 0, 2)) for x in (rows, cols, diag))
    up = lax.axis_index(UP)
    group = ((up ^ (up >> 1)) << 1) | lax.axis_index(ZHIGH)
    where = jnp.stack([group, lax.axis_index(CORE)]).astype(jnp.int32)
    hbm = pl.BlockSpec(memory_space=pltpu.HBM)
    return pl.pallas_call(
        functools.partial(load_kernel, chips, pieces),
        out_shape=(
            pltpu.VMEM(tiles.shape, tiles.dtype),
            pltpu.VMEM((terms + 1, 1, slots), jnp.int32),
        ),
        in_specs=[SMEM, pl.BlockSpec(memory_space=pl.ANY)] + [hbm] * 5,
        out_specs=(VMEM, VMEM),
        scratch_shapes=[
            pltpu.SMEM(counts.shape, jnp.int32),
            pltpu.VMEM((3, *rows.shape), jnp.int32),
            pltpu.SemaphoreType.DMA((terms, slots // GROUP)),
            pltpu.SemaphoreType.DMA((4,)),
        ],
        compiler_params=pltpu.CompilerParams(vmem_limit_bytes=1024 * 1024),
    )(
        where,
        after,
        *(
            pltpu.with_memory_space_constraint(x, pltpu.HBM)
            for x in (rows, cols, counts, diag, tiles)
        ),
    )


def for_slots(codes, tiles, work):
    terms, slots = tiles.shape[:2]
    for t in range(terms):
        count = codes[terms, 0, t]

        @pl.loop(0, (count + GROUP - 1) // GROUP)
        def _(g):
            outs = []
            for u in range(GROUP):
                k = g * GROUP + u
                outs.append(work(codes[t, 0, k], tiles[t, k]))
            for ref, at, value in outs:
                ref[at, pl.ds(t * value.shape[0], value.shape[0]), :] += value


def mirror_kernel(codes, row_segs, col_segs, tiles, mir, mir_away, sums):
    terms = tiles.shape[0]
    vecs = row_segs.shape[1]
    chips = mir.shape[0]
    span = terms * vecs
    sums[...] = jnp.zeros_like(sums)
    for_slots(
        codes,
        tiles,
        lambda code, w: (sums, (code >> 8) & 63, dot_rows(row_segs[code & 7], w)),
    )

    def products(seg, part):
        high = part.astype(jnp.bfloat16)
        low = (part - high.astype(jnp.float32)).astype(jnp.bfloat16)
        return dot_cols(seg, jnp.concatenate([high, low], axis=0))

    total = jnp.zeros((vecs, 2 * span), jnp.float32)
    for h, out in enumerate((mir, mir_away)):
        for s in range(chips):
            part = sums[h * chips + s]
            out[s, :span, :] = part
            total += products(col_segs[2 * s + h], part)
    square = products(row_segs[0], sums[2 * chips])
    small = jnp.concatenate(
        [
            total[:, :span] + total[:, span:],
            square[:, :span] + square[:, span:],
            jnp.zeros((vecs, mir.shape[2] - 2 * span), jnp.float32),
        ],
        axis=1,
    )
    for s in range(chips):
        mir[s, span:, :] = small
        mir_away[s, span:, :] = small


def forward_kernel(codes, col_segs, tiles, fwd, sums):
    span = sums.shape[1]
    sums[...] = jnp.zeros_like(sums)
    for_slots(
        codes,
        tiles,
        lambda code, w: (sums, code >> 14, dot_cols(col_segs[(code >> 3) & 31], w)),
    )
    fwd[:, :span, :] = sums[: fwd.shape[0]]
    fwd[:, span:, :] = jnp.zeros_like(fwd[:, span:, :])


def apply_mirror(codes, row_segs, col_segs, tiles):
    terms = tiles.shape[0]
    vecs, width = row_segs.shape[1:]
    chips = col_segs.shape[0] // 2
    out = pltpu.VMEM((chips, (terms + 1) * vecs, width), jnp.float32)
    return pl.pallas_call(
        mirror_kernel,
        out_shape=(out, out),
        in_specs=[SMEM] + [VMEM] * 3,
        out_specs=(VMEM, VMEM),
        scratch_shapes=[pltpu.VMEM((2 * chips + 2, terms * vecs, width), jnp.float32)],
        compiler_params=pltpu.CompilerParams(vmem_limit_bytes=4 * 1024 * 1024),
    )(codes, in_vmem(row_segs), in_vmem(col_segs), in_vmem(tiles))


def apply_forward(codes, col_segs, tiles, pieces):
    terms = tiles.shape[0]
    vecs, width = col_segs.shape[1:]
    return pl.pallas_call(
        forward_kernel,
        out_shape=pltpu.VMEM((pieces, (terms + 1) * vecs, width), jnp.float32),
        in_specs=[SMEM] + [VMEM] * 2,
        out_specs=VMEM,
        scratch_shapes=[pltpu.VMEM((pieces + 1, terms * vecs, width), jnp.float32)],
        compiler_params=pltpu.CompilerParams(vmem_limit_bytes=4 * 1024 * 1024),
    )(codes, in_vmem(col_segs), in_vmem(tiles))


def exchange(value, axis):
    return lax.all_to_all(value, axis, 0, 0, tiled=True)


def swap_pairs(value, axis):
    return lax.ppermute(value, axis, [(i, i ^ 1) for i in range(lax.axis_size(axis))])


def swap_ends(value, axis):
    last = lax.axis_size(axis) - 1
    return lax.ppermute(value, axis, [(i, last - i) for i in range(last + 1)])


def shards(vectors, tile_vals, tile_rows, tile_cols, tile_counts, tile_diag):
    vecs, width = vectors.shape
    terms = tile_vals.shape[2]
    span = terms * vecs
    chips = lax.axis_size(CHIPS)
    pieces = lax.axis_size(COL)

    beyond = swap_pairs(vectors[None], ZHIGH)
    pairs, own = spread(vectors, swap_pairs(vectors[None], CORE), chips)
    col_segs = exchange(pairs, CHIPS)
    row_segs = jnp.concatenate([own, beyond], axis=0)
    arrived = swap_pairs(row_segs, UP)
    tiles, codes = load_tiles(
        chips, pieces, beyond, tile_rows, tile_cols, tile_counts, tile_diag, tile_vals[0, 0]
    )
    row_segs = jnp.concatenate([row_segs, arrived], axis=0)
    row_segs, col_segs, codes, tiles = lax.optimization_barrier((row_segs, col_segs, codes, tiles))
    col_segs = col_segs.reshape(2 * chips, vecs, width)
    arrived = swap_ends(row_segs, UP)
    fwd = apply_forward(codes, col_segs, tiles, pieces)
    fwd, arrived = lax.optimization_barrier((fwd, arrived))
    row_segs = jnp.concatenate([row_segs, arrived], axis=0)

    mir, mir_away = apply_mirror(codes, row_segs, col_segs, tiles)
    mir = mir + swap_pairs(mir_away, CORE)
    mir = jnp.sum(exchange(mir, CHIPS), axis=0)
    fwd = lax.dynamic_update_slice(
        fwd, jnp.broadcast_to(mir[span:], (pieces, vecs, width)), (0, span, 0)
    )
    fwd = jnp.sum(exchange(fwd, COL), axis=0)
    applied = (fwd[:span] + mir[:span]).reshape(terms, vecs, width)
    small = fwd[span:, : 2 * span].reshape(vecs, 2, terms, vecs)
    small = small[:, 0].transpose(1, 0, 2) + (small[:, 0] + small[:, 1]).transpose(1, 2, 0)
    states = width * lax.axis_size(ROW) * lax.axis_size(COL)
    return applied, small / math.sqrt(states)


def solution(mesh):
    torus = Mesh(mesh.devices.reshape(4, 4, 2, 4, 2), ROW + COL)
    grid = P(ROW, COL)
    return jax.shard_map(
        shards,
        mesh=torus,
        in_specs=(P(None, ROW + COL), grid, grid, grid, grid, grid),
        out_specs=(P(None, None, ROW + COL), P()),
        check_vma=False,
    )
```

```python
import functools
import math

import jax
import jax.numpy as jnp
from jax import lax
from jax.experimental import pallas as pl
from jax.experimental.pallas import tpu as pltpu
from jax.sharding import Mesh
from jax.sharding import PartitionSpec as P

ZLOW, ACROSS, CORE, UP, ZHIGH = "zlow", "across", "core", "up", "zhigh"
ROW = (ZLOW, ACROSS, CORE)
CHIPS = (ZLOW, ACROSS)
COL = (UP, ZHIGH)
CHUNK = 8
SMEM = pl.BlockSpec(memory_space=pltpu.SMEM)
VMEM = pl.BlockSpec(memory_space=pltpu.VMEM)


def in_vmem(value):
    return pltpu.with_memory_space_constraint(value, pltpu.VMEM)


def dot_cols(x, w):
    return lax.dot_general(x, w, (((1,), (1,)), ((), ())), preferred_element_type=jnp.float32)


def dot_rows(x, w):
    return lax.dot_general(x, w, (((1,), (0,)), ((), ())), preferred_element_type=jnp.float32)


def keep_kernel(own, kept):
    kept[0] = own[...]


def keep(own):
    return pl.pallas_call(
        keep_kernel,
        out_shape=pltpu.VMEM((1, *own.shape), own.dtype),
        in_specs=[VMEM],
        out_specs=VMEM,
        compiler_params=pltpu.CompilerParams(vmem_limit_bytes=1024 * 1024),
    )(pltpu.with_memory_space_constraint(own, pltpu.HBM))


def spread_kernel(own, other, pairs):
    for s in range(pairs.shape[0]):
        pairs[s, 0] = own[0]
        pairs[s, 1] = other[0]


def spread(own, other, copies):
    return pl.pallas_call(
        spread_kernel,
        out_shape=pltpu.VMEM((copies, 2, *own.shape[1:]), own.dtype),
        in_specs=[VMEM] * 2,
        out_specs=VMEM,
        compiler_params=pltpu.CompilerParams(vmem_limit_bytes=1024 * 1024),
    )(in_vmem(own), in_vmem(other))


def load_kernel(
    chips, pieces, where, after, rows, cols, counts, diag, stored, tiles, codes, live, index, sems, done
):
    terms, slots = tiles.shape[:2]
    small = [
        pltpu.make_async_copy(counts, live, done.at[0]),
        pltpu.make_async_copy(rows, index.at[0], done.at[1]),
        pltpu.make_async_copy(cols, index.at[1], done.at[2]),
        pltpu.make_async_copy(diag, index.at[2], done.at[3]),
    ]
    large = []
    for t in range(terms):
        for g in range(slots // CHUNK):
            at = pl.ds(g * CHUNK, CHUNK)
            large.append(pltpu.make_async_copy(stored.at[t, at], tiles.at[t, at], sems.at[t, g]))
    for copy in small + large:
        copy.start()
    for copy in small:
        copy.wait()
    slot = lax.broadcasted_iota(jnp.int32, (1, slots), 1)
    for t in range(terms):
        row, col, same = (index[n, t] for n in range(3))
        used = slot < live[0, 0, t]
        near = row ^ ((row & 4) >> 1) ^ where[0]
        far = col ^ where[1]
        mirrored = jnp.where(same == 1, 2 * chips, (far & 1) * chips + (far >> 1))
        mirrored = jnp.where(used, mirrored, 2 * chips + 1)
        forward = jnp.where(used, row, pieces)
        codes[t] = near | (far << 3) | (mirrored << 8) | (forward << 14)
    for copy in large:
        copy.wait()


def load_tiles(chips, pieces, after, rows, cols, counts, diag, tiles):
    terms, slots = tiles.shape[:2]
    rows, cols, diag = (jnp.transpose(x[0], (1, 0, 2)) for x in (rows, cols, diag))
    up = lax.axis_index(UP)
    group = ((up ^ (up >> 1)) << 1) | lax.axis_index(ZHIGH)
    where = jnp.stack([group, lax.axis_index(CORE)]).astype(jnp.int32)
    hbm = pl.BlockSpec(memory_space=pltpu.HBM)
    return pl.pallas_call(
        functools.partial(load_kernel, chips, pieces),
        out_shape=(
            pltpu.VMEM(tiles.shape, tiles.dtype),
            pltpu.VMEM((terms, 1, slots), jnp.int32),
        ),
        in_specs=[SMEM, pl.BlockSpec(memory_space=pl.ANY)] + [hbm] * 5,
        out_specs=(VMEM, VMEM),
        scratch_shapes=[
            pltpu.SMEM(counts.shape, jnp.int32),
            pltpu.VMEM((3, *rows.shape), jnp.int32),
            pltpu.SemaphoreType.DMA((terms, slots // CHUNK)),
            pltpu.SemaphoreType.DMA((4,)),
        ],
        compiler_params=pltpu.CompilerParams(vmem_limit_bytes=1024 * 1024),
    )(
        where,
        after,
        *(
            pltpu.with_memory_space_constraint(x, pltpu.HBM)
            for x in (rows, cols, counts, diag, tiles)
        ),
    )


def for_slots(codes, tiles, work):
    terms, slots = tiles.shape[:2]
    for t in range(terms):
        outs = [work(codes[t, 0, k], tiles[t, k]) for k in range(slots)]
        for ref, at, value in outs:
            ref[at, pl.ds(t * value.shape[0], value.shape[0]), :] += value


def mirror_kernel(codes, row_segs, col_segs, tiles, mir, mir_away, sums):
    terms = tiles.shape[0]
    vecs = row_segs.shape[1]
    chips = mir.shape[0]
    span = terms * vecs
    sums[...] = jnp.zeros_like(sums)
    for_slots(
        codes,
        tiles,
        lambda code, w: (sums, (code >> 8) & 63, dot_rows(row_segs[code & 7], w)),
    )

    def products(seg, part):
        high = part.astype(jnp.bfloat16)
        low = (part - high.astype(jnp.float32)).astype(jnp.bfloat16)
        return dot_cols(seg, jnp.concatenate([high, low], axis=0))

    total = jnp.zeros((vecs, 2 * span), jnp.float32)
    for h, out in enumerate((mir, mir_away)):
        for s in range(chips):
            part = sums[h * chips + s]
            out[s, :span, :] = part
            total += products(col_segs[2 * s + h], part)
    square = products(row_segs[0], sums[2 * chips])
    small = jnp.concatenate(
        [
            total[:, :span] + total[:, span:],
            square[:, :span] + square[:, span:],
            jnp.zeros((vecs, mir.shape[2] - 2 * span), jnp.float32),
        ],
        axis=1,
    )
    for s in range(chips):
        mir[s, span:, :] = small
        mir_away[s, span:, :] = small


def forward_kernel(codes, col_segs, tiles, fwd, sums):
    span = sums.shape[1]
    sums[...] = jnp.zeros_like(sums)
    for_slots(
        codes,
        tiles,
        lambda code, w: (sums, code >> 14, dot_cols(col_segs[(code >> 3) & 31], w)),
    )
    fwd[:, :span, :] = sums[: fwd.shape[0]]
    fwd[:, span:, :] = jnp.zeros_like(fwd[:, span:, :])


def apply_mirror(codes, row_segs, col_segs, tiles):
    terms = tiles.shape[0]
    vecs, width = row_segs.shape[1:]
    chips = col_segs.shape[0] // 2
    out = pltpu.VMEM((chips, (terms + 1) * vecs, width), jnp.float32)
    return pl.pallas_call(
        mirror_kernel,
        out_shape=(out, out),
        in_specs=[SMEM] + [VMEM] * 3,
        out_specs=(VMEM, VMEM),
        scratch_shapes=[pltpu.VMEM((2 * chips + 2, terms * vecs, width), jnp.float32)],
        compiler_params=pltpu.CompilerParams(vmem_limit_bytes=4 * 1024 * 1024),
    )(codes, in_vmem(row_segs), in_vmem(col_segs), in_vmem(tiles))


def apply_forward(codes, col_segs, tiles, pieces):
    terms = tiles.shape[0]
    vecs, width = col_segs.shape[1:]
    return pl.pallas_call(
        forward_kernel,
        out_shape=pltpu.VMEM((pieces, (terms + 1) * vecs, width), jnp.float32),
        in_specs=[SMEM] + [VMEM] * 2,
        out_specs=VMEM,
        scratch_shapes=[pltpu.VMEM((pieces + 1, terms * vecs, width), jnp.float32)],
        compiler_params=pltpu.CompilerParams(vmem_limit_bytes=4 * 1024 * 1024),
    )(codes, in_vmem(col_segs), in_vmem(tiles))


def finish_kernel(states, came, mir, applied, small):
    terms, vecs = small.shape[:2]
    span = terms * vecs
    total = came[0]
    for p in range(1, came.shape[0]):
        total += came[p]
    applied[...] = total[:span] + mir[:span]
    mixed = total[span:] * (1.0 / math.sqrt(states))
    turned = jnp.transpose(mixed)
    for t in range(terms):
        at = t * vecs
        small[t] = mixed[:, at : at + vecs] + (
            turned[at : at + vecs] + turned[span + at : span + at + vecs]
        )


def finish(came, mir, terms, states):
    vecs, width = came.shape[1] // (terms + 1), came.shape[2]
    return pl.pallas_call(
        functools.partial(finish_kernel, states),
        out_shape=(
            jax.ShapeDtypeStruct((terms * vecs, width), jnp.float32),
            jax.ShapeDtypeStruct((terms, vecs, vecs), jnp.float32),
        ),
        in_specs=[VMEM] * 2,
        out_specs=(VMEM, VMEM),
        compiler_params=pltpu.CompilerParams(vmem_limit_bytes=1024 * 1024),
    )(in_vmem(came), in_vmem(mir))


def exchange(value, axis):
    return lax.all_to_all(value, axis, 0, 0, tiled=True)


def swap_pairs(value, axis):
    return lax.ppermute(value, axis, [(i, i ^ 1) for i in range(lax.axis_size(axis))])


def swap_ends(value, axis):
    last = lax.axis_size(axis) - 1
    return lax.ppermute(value, axis, [(i, last - i) for i in range(last + 1)])


def shards(vectors, tile_vals, tile_rows, tile_cols, tile_counts, tile_diag):
    vecs, width = vectors.shape
    terms = tile_vals.shape[2]
    span = terms * vecs
    chips = lax.axis_size(CHIPS)
    pieces = lax.axis_size(COL)

    beyond = swap_pairs(vectors[None], ZHIGH)
    own = keep(vectors)
    pairs = spread(own, swap_pairs(vectors[None], CORE), chips)
    pairs, own = lax.optimization_barrier((pairs, own))
    col_segs = exchange(pairs, CHIPS)
    row_segs = jnp.concatenate([own, beyond], axis=0)
    arrived = swap_pairs(row_segs, UP)
    tiles, codes = load_tiles(
        chips, pieces, beyond, tile_rows, tile_cols, tile_counts, tile_diag, tile_vals[0, 0]
    )
    row_segs = jnp.concatenate([row_segs, arrived], axis=0)
    row_segs, codes, tiles = lax.optimization_barrier((row_segs, codes, tiles))
    col_segs = col_segs.reshape(2 * chips, vecs, width)
    arrived = swap_ends(row_segs, UP)
    fwd = apply_forward(codes, col_segs, tiles, pieces)
    fwd, arrived = lax.optimization_barrier((fwd, arrived))
    row_segs = jnp.concatenate([row_segs, arrived], axis=0)

    mir, mir_away = apply_mirror(codes, row_segs, col_segs, tiles)
    mir = mir + swap_pairs(mir_away, CORE)
    mir = jnp.sum(exchange(mir, CHIPS), axis=0)
    fwd = lax.dynamic_update_slice(
        fwd, jnp.broadcast_to(mir[span:], (pieces, vecs, width)), (0, span, 0)
    )
    states = width * lax.axis_size(ROW) * lax.axis_size(COL)
    applied, small = finish(exchange(fwd, COL), mir, terms, states)
    return applied.reshape(terms, vecs, width), small


def solution(mesh):
    torus = Mesh(mesh.devices.reshape(4, 4, 2, 4, 2), ROW + COL)
    grid = P(ROW, COL)
    return jax.shard_map(
        shards,
        mesh=torus,
        in_specs=(P(None, ROW + COL), grid, grid, grid, grid, grid),
        out_specs=(P(None, None, ROW + COL), P()),
        check_vma=False,
    )
```

```python
import functools
import math

import jax
import jax.numpy as jnp
from jax import lax
from jax.experimental import pallas as pl
from jax.experimental.pallas import tpu as pltpu
from jax.sharding import Mesh
from jax.sharding import PartitionSpec as P

ZLOW, ACROSS, CORE, UP, ZHIGH = "zlow", "across", "core", "up", "zhigh"
ROW = (ZLOW, ACROSS, CORE)
CHIPS = (ZLOW, ACROSS)
COL = (UP, ZHIGH)
CHUNK = 8
SMEM = pl.BlockSpec(memory_space=pltpu.SMEM)
VMEM = pl.BlockSpec(memory_space=pltpu.VMEM)


def in_vmem(value):
    return pltpu.with_memory_space_constraint(value, pltpu.VMEM)


def dot_cols(x, w):
    return lax.dot_general(x, w, (((1,), (1,)), ((), ())), preferred_element_type=jnp.float32)


def dot_rows(x, w):
    return lax.dot_general(x, w, (((1,), (0,)), ((), ())), preferred_element_type=jnp.float32)


def keep_kernel(own, kept):
    kept[0] = own[...]


def keep(own):
    return pl.pallas_call(
        keep_kernel,
        out_shape=pltpu.VMEM((1, *own.shape), own.dtype),
        in_specs=[VMEM],
        out_specs=VMEM,
        compiler_params=pltpu.CompilerParams(vmem_limit_bytes=1024 * 1024),
    )(pltpu.with_memory_space_constraint(own, pltpu.HBM))


def spread_kernel(own, other, pairs):
    for s in range(pairs.shape[0]):
        pairs[s, 0] = own[0]
        pairs[s, 1] = other[0]


def spread(own, other, copies):
    return pl.pallas_call(
        spread_kernel,
        out_shape=pltpu.VMEM((copies, 2, *own.shape[1:]), own.dtype),
        in_specs=[VMEM] * 2,
        out_specs=VMEM,
        compiler_params=pltpu.CompilerParams(vmem_limit_bytes=1024 * 1024),
    )(in_vmem(own), in_vmem(other))


def load_kernel(
    chips, pieces, where, after, rows, cols, counts, diag, stored, tiles, codes, live, index, sems, done
):
    terms, slots = tiles.shape[:2]
    small = [
        pltpu.make_async_copy(counts, live, done.at[0]),
        pltpu.make_async_copy(rows, index.at[0], done.at[1]),
        pltpu.make_async_copy(cols, index.at[1], done.at[2]),
        pltpu.make_async_copy(diag, index.at[2], done.at[3]),
    ]
    large = []
    for t in range(terms):
        for g in range(slots // CHUNK):
            at = pl.ds(g * CHUNK, CHUNK)
            large.append(pltpu.make_async_copy(stored.at[t, at], tiles.at[t, at], sems.at[t, g]))
    for copy in small + large:
        copy.start()
    for copy in small:
        copy.wait()
    slot = lax.broadcasted_iota(jnp.int32, (1, slots), 1)
    for t in range(terms):
        row, col, same = (index[n, t] for n in range(3))
        used = slot < live[0, 0, t]
        near = row ^ ((row & 4) >> 1) ^ where[0]
        far = col ^ where[1]
        mirrored = jnp.where(same == 1, 2 * chips, (far & 1) * chips + (far >> 1))
        mirrored = jnp.where(used, mirrored, 2 * chips + 1)
        forward = jnp.where(used, row, pieces)
        codes[t] = near | (far << 3) | (mirrored << 8) | (forward << 14)
    codes[terms] = jnp.zeros((1, slots), jnp.int32) + where[0]
    for copy in large:
        copy.wait()


def load_tiles(chips, pieces, after, rows, cols, counts, diag, tiles):
    terms, slots = tiles.shape[:2]
    rows, cols, diag = (jnp.transpose(x[0], (1, 0, 2)) for x in (rows, cols, diag))
    up = lax.axis_index(UP)
    group = ((up ^ (up >> 1)) << 1) | lax.axis_index(ZHIGH)
    where = jnp.stack([group, lax.axis_index(CORE)]).astype(jnp.int32)
    hbm = pl.BlockSpec(memory_space=pltpu.HBM)
    return pl.pallas_call(
        functools.partial(load_kernel, chips, pieces),
        out_shape=(
            pltpu.VMEM(tiles.shape, tiles.dtype),
            pltpu.VMEM((terms + 1, 1, slots), jnp.int32),
        ),
        in_specs=[SMEM, pl.BlockSpec(memory_space=pl.ANY)] + [hbm] * 5,
        out_specs=(VMEM, VMEM),
        scratch_shapes=[
            pltpu.SMEM(counts.shape, jnp.int32),
            pltpu.VMEM((3, *rows.shape), jnp.int32),
            pltpu.SemaphoreType.DMA((terms, slots // CHUNK)),
            pltpu.SemaphoreType.DMA((4,)),
        ],
        compiler_params=pltpu.CompilerParams(vmem_limit_bytes=1024 * 1024),
    )(
        where,
        after,
        *(
            pltpu.with_memory_space_constraint(x, pltpu.HBM)
            for x in (rows, cols, counts, diag, tiles)
        ),
    )


def for_slots(codes, tiles, work):
    terms, slots = tiles.shape[:2]
    for t in range(terms):
        outs = [work(codes[t, 0, k], tiles[t, k]) for k in range(slots)]
        for ref, at, value in outs:
            ref[at, pl.ds(t * value.shape[0], value.shape[0]), :] += value


def mirror_kernel(codes, row_segs, fwd, tiles, mir, mir_away, sums):
    terms = tiles.shape[0]
    vecs = row_segs.shape[1]
    chips = mir.shape[0]
    span = terms * vecs
    sums[...] = jnp.zeros_like(sums)

    def products(seg, part):
        high = part.astype(jnp.bfloat16)
        low = (part - high.astype(jnp.float32)).astype(jnp.bfloat16)
        out = dot_cols(seg, jnp.concatenate([high, low], axis=0))
        return out[:, :span] + out[:, span:]

    group = codes[terms, 0, 0]
    total = jnp.zeros((vecs, span), jnp.float32)
    for a in range(fwd.shape[0]):
        total += products(row_segs[(a ^ ((a & 4) >> 1)) ^ group], fwd[a, :span, :])
    for_slots(
        codes,
        tiles,
        lambda code, w: (sums, (code >> 8) & 63, dot_rows(row_segs[code & 7], w)),
    )
    small = jnp.concatenate(
        [
            total,
            products(row_segs[0], sums[2 * chips]),
            jnp.zeros((vecs, mir.shape[2] - 2 * span), jnp.float32),
        ],
        axis=1,
    )
    for s in range(chips):
        mir[s, :span, :] = sums[s]
        mir[s, span:, :] = small
        mir_away[s, :span, :] = sums[chips + s]
        mir_away[s, span:, :] = small


def forward_kernel(codes, col_segs, tiles, fwd, sums):
    span = sums.shape[1]
    sums[...] = jnp.zeros_like(sums)
    for_slots(
        codes,
        tiles,
        lambda code, w: (sums, code >> 14, dot_cols(col_segs[(code >> 3) & 31], w)),
    )
    fwd[:, :span, :] = sums[: fwd.shape[0]]
    fwd[:, span:, :] = jnp.zeros_like(fwd[:, span:, :])


def apply_mirror(codes, row_segs, fwd, tiles, chips):
    terms = tiles.shape[0]
    vecs, width = row_segs.shape[1:]
    out = pltpu.VMEM((chips, (terms + 1) * vecs, width), jnp.float32)
    return pl.pallas_call(
        mirror_kernel,
        out_shape=(out, out),
        in_specs=[SMEM] + [VMEM] * 3,
        out_specs=(VMEM, VMEM),
        scratch_shapes=[pltpu.VMEM((2 * chips + 2, terms * vecs, width), jnp.float32)],
        compiler_params=pltpu.CompilerParams(vmem_limit_bytes=4 * 1024 * 1024),
    )(codes, in_vmem(row_segs), in_vmem(fwd), in_vmem(tiles))


def apply_forward(codes, col_segs, tiles, pieces):
    terms = tiles.shape[0]
    vecs, width = col_segs.shape[1:]
    return pl.pallas_call(
        forward_kernel,
        out_shape=pltpu.VMEM((pieces, (terms + 1) * vecs, width), jnp.float32),
        in_specs=[SMEM] + [VMEM] * 2,
        out_specs=VMEM,
        scratch_shapes=[pltpu.VMEM((pieces + 1, terms * vecs, width), jnp.float32)],
        compiler_params=pltpu.CompilerParams(vmem_limit_bytes=4 * 1024 * 1024),
    )(codes, in_vmem(col_segs), in_vmem(tiles))


def finish_kernel(states, came, mir, applied, small):
    terms, vecs = small.shape[:2]
    span = terms * vecs
    total = came[0]
    for p in range(1, came.shape[0]):
        total += came[p]
    applied[...] = total[:span] + mir[:span]
    mixed = total[span:] * (1.0 / math.sqrt(states))
    turned = jnp.transpose(mixed)
    for t in range(terms):
        at = t * vecs
        small[t] = (
            mixed[:, at : at + vecs]
            + turned[at : at + vecs]
            - mixed[:, span + at : span + at + vecs]
        )


def finish(came, mir, terms, states):
    vecs, width = came.shape[1] // (terms + 1), came.shape[2]
    return pl.pallas_call(
        functools.partial(finish_kernel, states),
        out_shape=(
            jax.ShapeDtypeStruct((terms * vecs, width), jnp.float32),
            jax.ShapeDtypeStruct((terms, vecs, vecs), jnp.float32),
        ),
        in_specs=[VMEM] * 2,
        out_specs=(VMEM, VMEM),
        compiler_params=pltpu.CompilerParams(vmem_limit_bytes=1024 * 1024),
    )(in_vmem(came), in_vmem(mir))


def exchange(value, axis):
    return lax.all_to_all(value, axis, 0, 0, tiled=True)


def swap_pairs(value, axis):
    return lax.ppermute(value, axis, [(i, i ^ 1) for i in range(lax.axis_size(axis))])


def swap_ends(value, axis):
    last = lax.axis_size(axis) - 1
    return lax.ppermute(value, axis, [(i, last - i) for i in range(last + 1)])


def shards(vectors, tile_vals, tile_rows, tile_cols, tile_counts, tile_diag):
    vecs, width = vectors.shape
    terms = tile_vals.shape[2]
    span = terms * vecs
    chips = lax.axis_size(CHIPS)
    pieces = lax.axis_size(COL)

    beyond = swap_pairs(vectors[None], ZHIGH)
    own = keep(vectors)
    pairs = spread(own, swap_pairs(vectors[None], CORE), chips)
    pairs, own = lax.optimization_barrier((pairs, own))
    col_segs = exchange(pairs, CHIPS)
    row_segs = jnp.concatenate([own, beyond], axis=0)
    arrived = swap_pairs(row_segs, UP)
    tiles, codes = load_tiles(
        chips, pieces, beyond, tile_rows, tile_cols, tile_counts, tile_diag, tile_vals[0, 0]
    )
    row_segs = jnp.concatenate([row_segs, arrived], axis=0)
    row_segs, codes, tiles = lax.optimization_barrier((row_segs, codes, tiles))
    col_segs = col_segs.reshape(2 * chips, vecs, width)
    arrived = swap_ends(row_segs, UP)
    fwd = apply_forward(codes, col_segs, tiles, pieces)
    fwd, arrived = lax.optimization_barrier((fwd, arrived))
    row_segs = jnp.concatenate([row_segs, arrived], axis=0)

    mir, mir_away = apply_mirror(codes, row_segs, fwd, tiles, chips)
    mir = mir + swap_pairs(mir_away, CORE)
    mir = jnp.sum(exchange(mir, CHIPS), axis=0)
    fwd = lax.dynamic_update_slice(
        fwd, jnp.broadcast_to(mir[span:], (pieces, vecs, width)), (0, span, 0)
    )
    states = width * lax.axis_size(ROW) * lax.axis_size(COL)
    applied, small = finish(exchange(fwd, COL), mir, terms, states)
    return applied.reshape(terms, vecs, width), small


def solution(mesh):
    torus = Mesh(mesh.devices.reshape(4, 4, 2, 4, 2), ROW + COL)
    grid = P(ROW, COL)
    return jax.shard_map(
        shards,
        mesh=torus,
        in_specs=(P(None, ROW + COL), grid, grid, grid, grid, grid),
        out_specs=(P(None, None, ROW + COL), P()),
        check_vma=False,
    )
```

```python
import functools
import math

import jax
import jax.numpy as jnp
from jax import lax
from jax.experimental import pallas as pl
from jax.experimental.pallas import tpu as pltpu
from jax.sharding import Mesh
from jax.sharding import PartitionSpec as P

ZLOW, ACROSS, CORE, UP, ZHIGH = "zlow", "across", "core", "up", "zhigh"
ROW = (ZLOW, ACROSS, CORE)
CHIPS = (ZLOW, ACROSS)
COL = (UP, ZHIGH)
CHUNK = 8
SMEM = pl.BlockSpec(memory_space=pltpu.SMEM)
VMEM = pl.BlockSpec(memory_space=pltpu.VMEM)


def in_vmem(value):
    return pltpu.with_memory_space_constraint(value, pltpu.VMEM)


def dot_cols(x, w):
    return lax.dot_general(x, w, (((1,), (1,)), ((), ())), preferred_element_type=jnp.float32)


def dot_rows(x, w):
    return lax.dot_general(x, w, (((1,), (0,)), ((), ())), preferred_element_type=jnp.float32)


def keep_kernel(own, kept):
    kept[0] = own[...]


def keep(own):
    return pl.pallas_call(
        keep_kernel,
        out_shape=pltpu.VMEM((1, *own.shape), own.dtype),
        in_specs=[VMEM],
        out_specs=VMEM,
        compiler_params=pltpu.CompilerParams(vmem_limit_bytes=1024 * 1024),
    )(pltpu.with_memory_space_constraint(own, pltpu.HBM))


def spread_kernel(own, other, pairs):
    for s in range(pairs.shape[0]):
        pairs[s, 0] = own[0]
        pairs[s, 1] = other[0]


def spread(own, other, copies):
    return pl.pallas_call(
        spread_kernel,
        out_shape=pltpu.VMEM((copies, 2, *own.shape[1:]), own.dtype),
        in_specs=[VMEM] * 2,
        out_specs=VMEM,
        compiler_params=pltpu.CompilerParams(vmem_limit_bytes=1024 * 1024),
    )(in_vmem(own), in_vmem(other))


def load_kernel(
    chips, pieces, where, after, rows, cols, counts, diag, stored, tiles, codes, live, index, sems, done
):
    terms, slots = tiles.shape[:2]
    small = [
        pltpu.make_async_copy(counts, live, done.at[0]),
        pltpu.make_async_copy(rows, index.at[0], done.at[1]),
        pltpu.make_async_copy(cols, index.at[1], done.at[2]),
        pltpu.make_async_copy(diag, index.at[2], done.at[3]),
    ]
    large = []
    for t in range(terms):
        for g in range(slots // CHUNK):
            at = pl.ds(g * CHUNK, CHUNK)
            large.append(pltpu.make_async_copy(stored.at[t, at], tiles.at[t, at], sems.at[t, g]))
    for copy in small + large:
        copy.start()
    for copy in small:
        copy.wait()
    slot = lax.broadcasted_iota(jnp.int32, (1, slots), 1)
    for t in range(terms):
        row, col, same = (index[n, t] for n in range(3))
        used = slot < live[0, 0, t]
        near = row ^ ((row & 4) >> 1) ^ where[0]
        far = col ^ where[1]
        mirrored = jnp.where(same == 1, 2 * chips, (far & 1) * chips + (far >> 1))
        mirrored = jnp.where(used, mirrored, 2 * chips + 1)
        forward = jnp.where(used, row, pieces)
        codes[t] = near | (far << 3) | (mirrored << 8) | (forward << 14)
    codes[terms] = jnp.zeros((1, slots), jnp.int32) + where[0]
    for copy in large:
        copy.wait()


def load_tiles(chips, pieces, after, rows, cols, counts, diag, tiles):
    terms, slots = tiles.shape[:2]
    rows, cols, diag = (jnp.transpose(x[0], (1, 0, 2)) for x in (rows, cols, diag))
    up = lax.axis_index(UP)
    group = ((up ^ (up >> 1)) << 1) | lax.axis_index(ZHIGH)
    where = jnp.stack([group, lax.axis_index(CORE)]).astype(jnp.int32)
    hbm = pl.BlockSpec(memory_space=pltpu.HBM)
    return pl.pallas_call(
        functools.partial(load_kernel, chips, pieces),
        out_shape=(
            pltpu.VMEM(tiles.shape, tiles.dtype),
            pltpu.VMEM((terms + 1, 1, slots), jnp.int32),
        ),
        in_specs=[SMEM, pl.BlockSpec(memory_space=pl.ANY)] + [hbm] * 5,
        out_specs=(VMEM, VMEM),
        scratch_shapes=[
            pltpu.SMEM(counts.shape, jnp.int32),
            pltpu.VMEM((3, *rows.shape), jnp.int32),
            pltpu.SemaphoreType.DMA((terms, slots // CHUNK)),
            pltpu.SemaphoreType.DMA((4,)),
        ],
        compiler_params=pltpu.CompilerParams(vmem_limit_bytes=1024 * 1024),
    )(
        where,
        after,
        *(
            pltpu.with_memory_space_constraint(x, pltpu.HBM)
            for x in (rows, cols, counts, diag, tiles)
        ),
    )


def for_slots(codes, tiles, sums, work):
    terms, slots = tiles.shape[:2]
    for t in range(terms):
        outs = []
        for k in range(0, slots, 2):
            ats, values = work([codes[t, 0, k + n] for n in range(2)], tiles[t, k], tiles[t, k + 1])
            half = values.shape[0] // 2
            outs += [(ats[0], values[:half]), (ats[1], values[half:])]
        for at, value in outs:
            sums[at, pl.ds(t * value.shape[0], value.shape[0]), :] += value


def paired(first, second):
    none = jnp.zeros_like(first)
    return jnp.concatenate(
        [jnp.concatenate([first, none], axis=1), jnp.concatenate([none, second], axis=1)], axis=0
    )


def mirror_kernel(codes, row_segs, fwd, tiles, mir, mir_away, sums):
    terms = tiles.shape[0]
    vecs = row_segs.shape[1]
    chips = mir.shape[0]
    span = terms * vecs
    sums[...] = jnp.zeros_like(sums)

    def products(seg, part):
        high = part.astype(jnp.bfloat16)
        low = (part - high.astype(jnp.float32)).astype(jnp.bfloat16)
        out = dot_cols(seg, jnp.concatenate([high, low], axis=0))
        return out[:, :span] + out[:, span:]

    group = codes[terms, 0, 0]
    total = jnp.zeros((vecs, span), jnp.float32)
    for a in range(fwd.shape[0]):
        total += products(row_segs[(a ^ ((a & 4) >> 1)) ^ group], fwd[a, :span, :])

    def work(pair, w, v):
        both = paired(*(row_segs[code & 7] for code in pair))
        out = dot_rows(both, jnp.concatenate([w, v], axis=0))
        return [(code >> 8) & 63 for code in pair], out

    for_slots(codes, tiles, sums, work)
    small = jnp.concatenate(
        [
            total,
            products(row_segs[0], sums[2 * chips]),
            jnp.zeros((vecs, mir.shape[2] - 2 * span), jnp.float32),
        ],
        axis=1,
    )
    for s in range(chips):
        mir[s, :span, :] = sums[s]
        mir[s, span:, :] = small
        mir_away[s, :span, :] = sums[chips + s]
        mir_away[s, span:, :] = small


def forward_kernel(codes, col_segs, tiles, fwd, sums):
    span = sums.shape[1]
    sums[...] = jnp.zeros_like(sums)

    def work(pair, w, v):
        both = paired(*(col_segs[(code >> 3) & 31] for code in pair))
        out = dot_cols(both, jnp.concatenate([w, v], axis=1))
        return [code >> 14 for code in pair], out

    for_slots(codes, tiles, sums, work)
    fwd[:, :span, :] = sums[: fwd.shape[0]]
    fwd[:, span:, :] = jnp.zeros_like(fwd[:, span:, :])


def apply_mirror(codes, row_segs, fwd, tiles, chips):
    terms = tiles.shape[0]
    vecs, width = row_segs.shape[1:]
    out = pltpu.VMEM((chips, (terms + 1) * vecs, width), jnp.float32)
    return pl.pallas_call(
        mirror_kernel,
        out_shape=(out, out),
        in_specs=[SMEM] + [VMEM] * 3,
        out_specs=(VMEM, VMEM),
        scratch_shapes=[pltpu.VMEM((2 * chips + 2, terms * vecs, width), jnp.float32)],
        compiler_params=pltpu.CompilerParams(vmem_limit_bytes=4 * 1024 * 1024),
    )(codes, in_vmem(row_segs), in_vmem(fwd), in_vmem(tiles))


def apply_forward(codes, col_segs, tiles, pieces):
    terms = tiles.shape[0]
    vecs, width = col_segs.shape[1:]
    return pl.pallas_call(
        forward_kernel,
        out_shape=pltpu.VMEM((pieces, (terms + 1) * vecs, width), jnp.float32),
        in_specs=[SMEM] + [VMEM] * 2,
        out_specs=VMEM,
        scratch_shapes=[pltpu.VMEM((pieces + 1, terms * vecs, width), jnp.float32)],
        compiler_params=pltpu.CompilerParams(vmem_limit_bytes=4 * 1024 * 1024),
    )(codes, in_vmem(col_segs), in_vmem(tiles))


def finish_kernel(states, came, mir, applied, small):
    terms, vecs = small.shape[:2]
    span = terms * vecs
    total = came[0]
    for p in range(1, came.shape[0]):
        total += came[p]
    applied[...] = total[:span] + mir[:span]
    mixed = total[span:] * (1.0 / math.sqrt(states))
    turned = jnp.transpose(mixed)
    for t in range(terms):
        at = t * vecs
        small[t] = (
            mixed[:, at : at + vecs]
            + turned[at : at + vecs]
            - mixed[:, span + at : span + at + vecs]
        )


def finish(came, mir, terms, states):
    vecs, width = came.shape[1] // (terms + 1), came.shape[2]
    return pl.pallas_call(
        functools.partial(finish_kernel, states),
        out_shape=(
            jax.ShapeDtypeStruct((terms * vecs, width), jnp.float32),
            jax.ShapeDtypeStruct((terms, vecs, vecs), jnp.float32),
        ),
        in_specs=[VMEM] * 2,
        out_specs=(VMEM, VMEM),
        compiler_params=pltpu.CompilerParams(vmem_limit_bytes=1024 * 1024),
    )(in_vmem(came), in_vmem(mir))


def exchange(value, axis):
    return lax.all_to_all(value, axis, 0, 0, tiled=True)


def swap_pairs(value, axis):
    return lax.ppermute(value, axis, [(i, i ^ 1) for i in range(lax.axis_size(axis))])


def swap_ends(value, axis):
    last = lax.axis_size(axis) - 1
    return lax.ppermute(value, axis, [(i, last - i) for i in range(last + 1)])


def shards(vectors, tile_vals, tile_rows, tile_cols, tile_counts, tile_diag):
    vecs, width = vectors.shape
    terms = tile_vals.shape[2]
    span = terms * vecs
    chips = lax.axis_size(CHIPS)
    pieces = lax.axis_size(COL)

    beyond = swap_pairs(vectors[None], ZHIGH)
    own = keep(vectors)
    pairs = spread(own, swap_pairs(vectors[None], CORE), chips)
    pairs, own = lax.optimization_barrier((pairs, own))
    col_segs = exchange(pairs, CHIPS)
    row_segs = jnp.concatenate([own, beyond], axis=0)
    arrived = swap_pairs(row_segs, UP)
    tiles, codes = load_tiles(
        chips, pieces, beyond, tile_rows, tile_cols, tile_counts, tile_diag, tile_vals[0, 0]
    )
    row_segs = jnp.concatenate([row_segs, arrived], axis=0)
    row_segs, codes, tiles = lax.optimization_barrier((row_segs, codes, tiles))
    col_segs = col_segs.reshape(2 * chips, vecs, width)
    arrived = swap_ends(row_segs, UP)
    fwd = apply_forward(codes, col_segs, tiles, pieces)
    fwd, arrived = lax.optimization_barrier((fwd, arrived))
    row_segs = jnp.concatenate([row_segs, arrived], axis=0)

    mir, mir_away = apply_mirror(codes, row_segs, fwd, tiles, chips)
    mir = mir + swap_pairs(mir_away, CORE)
    mir = jnp.sum(exchange(mir, CHIPS), axis=0)
    fwd = lax.dynamic_update_slice(
        fwd, jnp.broadcast_to(mir[span:], (pieces, vecs, width)), (0, span, 0)
    )
    states = width * lax.axis_size(ROW) * lax.axis_size(COL)
    applied, small = finish(exchange(fwd, COL), mir, terms, states)
    return applied.reshape(terms, vecs, width), small


def solution(mesh):
    torus = Mesh(mesh.devices.reshape(4, 4, 2, 4, 2), ROW + COL)
    grid = P(ROW, COL)
    return jax.shard_map(
        shards,
        mesh=torus,
        in_specs=(P(None, ROW + COL), grid, grid, grid, grid, grid),
        out_specs=(P(None, None, ROW + COL), P()),
        check_vma=False,
    )
```

```python
import functools
import math

import jax
import jax.numpy as jnp
from jax import lax
from jax.experimental import pallas as pl
from jax.experimental.pallas import tpu as pltpu
from jax.sharding import Mesh
from jax.sharding import PartitionSpec as P

ZLOW, ACROSS, CORE, UP, ZHIGH = "zlow", "across", "core", "up", "zhigh"
ROW = (ZLOW, ACROSS, CORE)
CHIPS = (ZLOW, ACROSS)
COL = (UP, ZHIGH)
CHUNK = 32
SMEM = pl.BlockSpec(memory_space=pltpu.SMEM)
VMEM = pl.BlockSpec(memory_space=pltpu.VMEM)


def in_vmem(value):
    return pltpu.with_memory_space_constraint(value, pltpu.VMEM)


def dot_cols(x, w):
    return lax.dot_general(x, w, (((1,), (1,)), ((), ())), preferred_element_type=jnp.float32)


def dot_rows(x, w):
    return lax.dot_general(x, w, (((1,), (0,)), ((), ())), preferred_element_type=jnp.float32)


def keep_kernel(own, kept):
    kept[0] = own[...]


def keep(own):
    return pl.pallas_call(
        keep_kernel,
        out_shape=pltpu.VMEM((1, *own.shape), own.dtype),
        in_specs=[VMEM],
        out_specs=VMEM,
        compiler_params=pltpu.CompilerParams(vmem_limit_bytes=1024 * 1024),
    )(pltpu.with_memory_space_constraint(own, pltpu.HBM))


def spread_kernel(own, other, pairs):
    for s in range(pairs.shape[0]):
        pairs[s, 0] = own[0]
        pairs[s, 1] = other[0]


def spread(own, other, copies):
    return pl.pallas_call(
        spread_kernel,
        out_shape=pltpu.VMEM((copies, 2, *own.shape[1:]), own.dtype),
        in_specs=[VMEM] * 2,
        out_specs=VMEM,
        compiler_params=pltpu.CompilerParams(vmem_limit_bytes=1024 * 1024),
    )(in_vmem(own), in_vmem(other))


def load_kernel(
    chips, pieces, where, after, rows, cols, counts, diag, stored, tiles, codes, live, index, sems, done
):
    terms, slots = tiles.shape[:2]
    small = [
        pltpu.make_async_copy(counts, live, done.at[0]),
        pltpu.make_async_copy(rows, index.at[0], done.at[1]),
        pltpu.make_async_copy(cols, index.at[1], done.at[2]),
        pltpu.make_async_copy(diag, index.at[2], done.at[3]),
    ]
    large = []
    for t in range(terms):
        for g in range(slots // CHUNK):
            at = pl.ds(g * CHUNK, CHUNK)
            large.append(pltpu.make_async_copy(stored.at[t, at], tiles.at[t, at], sems.at[t, g]))
    for copy in small + large:
        copy.start()
    for copy in small:
        copy.wait()
    slot = lax.broadcasted_iota(jnp.int32, (1, slots), 1)
    for t in range(terms):
        row, col, same = (index[n, t] for n in range(3))
        used = slot < live[0, 0, t]
        near = row ^ ((row & 4) >> 1) ^ where[0]
        far = col ^ where[1]
        mirrored = jnp.where(same == 1, 2 * chips, (far & 1) * chips + (far >> 1))
        mirrored = jnp.where(used, mirrored, 2 * chips + 1)
        forward = jnp.where(used, row, pieces)
        codes[t] = near | (far << 3) | (mirrored << 8) | (forward << 14)
    codes[terms] = jnp.zeros((1, slots), jnp.int32) + where[0]
    for copy in large:
        copy.wait()


def load_tiles(chips, pieces, after, rows, cols, counts, diag, tiles):
    terms, slots = tiles.shape[:2]
    rows, cols, diag = (jnp.transpose(x[0], (1, 0, 2)) for x in (rows, cols, diag))
    up = lax.axis_index(UP)
    group = ((up ^ (up >> 1)) << 1) | lax.axis_index(ZHIGH)
    where = jnp.stack([group, lax.axis_index(CORE)]).astype(jnp.int32)
    hbm = pl.BlockSpec(memory_space=pltpu.HBM)
    return pl.pallas_call(
        functools.partial(load_kernel, chips, pieces),
        out_shape=(
            pltpu.VMEM(tiles.shape, tiles.dtype),
            pltpu.VMEM((terms + 1, 1, slots), jnp.int32),
        ),
        in_specs=[SMEM, pl.BlockSpec(memory_space=pl.ANY)] + [hbm] * 5,
        out_specs=(VMEM, VMEM),
        scratch_shapes=[
            pltpu.SMEM(counts.shape, jnp.int32),
            pltpu.VMEM((3, *rows.shape), jnp.int32),
            pltpu.SemaphoreType.DMA((terms, slots // CHUNK)),
            pltpu.SemaphoreType.DMA((4,)),
        ],
        compiler_params=pltpu.CompilerParams(vmem_limit_bytes=1024 * 1024),
    )(
        where,
        after,
        *(
            pltpu.with_memory_space_constraint(x, pltpu.HBM)
            for x in (rows, cols, counts, diag, tiles)
        ),
    )


def for_slots(codes, tiles, sums, work):
    terms, slots = tiles.shape[:2]
    for t in range(terms):
        outs = []
        for k in range(0, slots, 2):
            ats, values = work([codes[t, 0, k + n] for n in range(2)], tiles[t, k], tiles[t, k + 1])
            half = values.shape[0] // 2
            outs += [(ats[0], values[:half]), (ats[1], values[half:])]
        for at, value in outs:
            sums[at, pl.ds(t * value.shape[0], value.shape[0]), :] += value


def paired(first, second):
    none = jnp.zeros_like(first)
    return jnp.concatenate(
        [jnp.concatenate([first, none], axis=1), jnp.concatenate([none, second], axis=1)], axis=0
    )


def mirror_kernel(codes, row_segs, fwd, tiles, mir, mir_away, sums):
    terms = tiles.shape[0]
    vecs = row_segs.shape[1]
    chips = mir.shape[0]
    span = terms * vecs
    sums[...] = jnp.zeros_like(sums)

    def products(seg, part):
        high = part.astype(jnp.bfloat16)
        low = (part - high.astype(jnp.float32)).astype(jnp.bfloat16)
        out = dot_cols(seg, jnp.concatenate([high, low], axis=0))
        return out[:, :span] + out[:, span:]

    group = codes[terms, 0, 0]
    total = jnp.zeros((vecs, span), jnp.float32)
    for a in range(fwd.shape[0]):
        total += products(row_segs[(a ^ ((a & 4) >> 1)) ^ group], fwd[a, :span, :])

    def work(pair, w, v):
        both = paired(*(row_segs[code & 7] for code in pair))
        out = dot_rows(both, jnp.concatenate([w, v], axis=0))
        return [(code >> 8) & 63 for code in pair], out

    for_slots(codes, tiles, sums, work)
    small = jnp.concatenate(
        [
            total,
            products(row_segs[0], sums[2 * chips]),
            jnp.zeros((vecs, mir.shape[2] - 2 * span), jnp.float32),
        ],
        axis=1,
    )
    for s in range(chips):
        mir[s, :span, :] = sums[s]
        mir[s, span:, :] = small
        mir_away[s, :span, :] = sums[chips + s]
        mir_away[s, span:, :] = small


def forward_kernel(codes, col_segs, tiles, fwd, sums):
    span = sums.shape[1]
    sums[...] = jnp.zeros_like(sums)

    def work(pair, w, v):
        both = paired(*(col_segs[(code >> 3) & 31] for code in pair))
        out = dot_cols(both, jnp.concatenate([w, v], axis=1))
        return [code >> 14 for code in pair], out

    for_slots(codes, tiles, sums, work)
    fwd[:, :span, :] = sums[: fwd.shape[0]]
    fwd[:, span:, :] = jnp.zeros_like(fwd[:, span:, :])


def apply_mirror(codes, row_segs, fwd, tiles, chips):
    terms = tiles.shape[0]
    vecs, width = row_segs.shape[1:]
    out = pltpu.VMEM((chips, (terms + 1) * vecs, width), jnp.float32)
    return pl.pallas_call(
        mirror_kernel,
        out_shape=(out, out),
        in_specs=[SMEM] + [VMEM] * 3,
        out_specs=(VMEM, VMEM),
        scratch_shapes=[pltpu.VMEM((2 * chips + 2, terms * vecs, width), jnp.float32)],
        compiler_params=pltpu.CompilerParams(vmem_limit_bytes=4 * 1024 * 1024),
    )(codes, in_vmem(row_segs), in_vmem(fwd), in_vmem(tiles))


def apply_forward(codes, col_segs, tiles, pieces):
    terms = tiles.shape[0]
    vecs, width = col_segs.shape[1:]
    return pl.pallas_call(
        forward_kernel,
        out_shape=pltpu.VMEM((pieces, (terms + 1) * vecs, width), jnp.float32),
        in_specs=[SMEM] + [VMEM] * 2,
        out_specs=VMEM,
        scratch_shapes=[pltpu.VMEM((pieces + 1, terms * vecs, width), jnp.float32)],
        compiler_params=pltpu.CompilerParams(vmem_limit_bytes=4 * 1024 * 1024),
    )(codes, in_vmem(col_segs), in_vmem(tiles))


def finish_kernel(states, came, mir, applied, small):
    terms, vecs = small.shape[:2]
    span = terms * vecs
    total = came[0]
    for p in range(1, came.shape[0]):
        total += came[p]
    applied[...] = total[:span] + mir[:span]
    mixed = total[span:] * (1.0 / math.sqrt(states))
    turned = jnp.transpose(mixed)
    for t in range(terms):
        at = t * vecs
        small[t] = (
            mixed[:, at : at + vecs]
            + turned[at : at + vecs]
            - mixed[:, span + at : span + at + vecs]
        )


def finish(came, mir, terms, states):
    vecs, width = came.shape[1] // (terms + 1), came.shape[2]
    return pl.pallas_call(
        functools.partial(finish_kernel, states),
        out_shape=(
            jax.ShapeDtypeStruct((terms * vecs, width), jnp.float32),
            jax.ShapeDtypeStruct((terms, vecs, vecs), jnp.float32),
        ),
        in_specs=[VMEM] * 2,
        out_specs=(VMEM, VMEM),
        compiler_params=pltpu.CompilerParams(vmem_limit_bytes=1024 * 1024),
    )(in_vmem(came), in_vmem(mir))


def exchange(value, axis):
    return lax.all_to_all(value, axis, 0, 0, tiled=True)


def swap_pairs(value, axis):
    return lax.ppermute(value, axis, [(i, i ^ 1) for i in range(lax.axis_size(axis))])


def swap_ends(value, axis):
    last = lax.axis_size(axis) - 1
    return lax.ppermute(value, axis, [(i, last - i) for i in range(last + 1)])


def shards(vectors, tile_vals, tile_rows, tile_cols, tile_counts, tile_diag):
    vecs, width = vectors.shape
    terms = tile_vals.shape[2]
    span = terms * vecs
    chips = lax.axis_size(CHIPS)
    pieces = lax.axis_size(COL)

    beyond = swap_pairs(vectors[None], ZHIGH)
    own = keep(vectors)
    pairs = spread(own, swap_pairs(vectors[None], CORE), chips)
    pairs, own = lax.optimization_barrier((pairs, own))
    col_segs = exchange(pairs, CHIPS)
    row_segs = jnp.concatenate([own, beyond], axis=0)
    arrived = swap_pairs(row_segs, UP)
    tiles, codes = load_tiles(
        chips, pieces, beyond, tile_rows, tile_cols, tile_counts, tile_diag, tile_vals[0, 0]
    )
    row_segs = jnp.concatenate([row_segs, arrived], axis=0)
    row_segs, codes, tiles = lax.optimization_barrier((row_segs, codes, tiles))
    col_segs = col_segs.reshape(2 * chips, vecs, width)
    arrived = swap_ends(row_segs, UP)
    fwd = apply_forward(codes, col_segs, tiles, pieces)
    fwd, arrived = lax.optimization_barrier((fwd, arrived))
    row_segs = jnp.concatenate([row_segs, arrived], axis=0)

    mir, mir_away = apply_mirror(codes, row_segs, fwd, tiles, chips)
    mir = mir + swap_pairs(mir_away, CORE)
    mir = jnp.sum(exchange(mir, CHIPS), axis=0)
    fwd = lax.dynamic_update_slice(
        fwd, jnp.broadcast_to(mir[span:], (pieces, vecs, width)), (0, span, 0)
    )
    states = width * lax.axis_size(ROW) * lax.axis_size(COL)
    applied, small = finish(exchange(fwd, COL), mir, terms, states)
    return applied.reshape(terms, vecs, width), small


def solution(mesh):
    torus = Mesh(mesh.devices.reshape(4, 4, 2, 4, 2), ROW + COL)
    grid = P(ROW, COL)
    return jax.shard_map(
        shards,
        mesh=torus,
        in_specs=(P(None, ROW + COL), grid, grid, grid, grid, grid),
        out_specs=(P(None, None, ROW + COL), P()),
        check_vma=False,
    )
```
